256 devices in a mesh: grp: 4 (over x), dev: 64 (over y, z, core).
Axes of the slice: x: 4, y: 4, z: 8, core: 2. Of those that a mesh axis runs over, the one named last changes fastest.
Arguments:
- nodes: bfloat16 [98304, 512], P(('grp', 'dev')), may hold values from -6 to 6
- senders: int32 [589824], P(('grp', 'dev')), may hold values from 0 to 1151
- mid_nodes: bfloat16 [24576, 512], P(('grp', 'dev')), may hold values from -6 to 6
- owners: int32 [98304, 1], P(('grp', 'dev')), may hold values from 0 to 63; in each aligned block of 384 rows (0 to 383, 384 to 767, ...) at most 12 rows name the same one
- slots: int32 [98304], P(('grp', 'dev')), may hold values from 0 to 95
- edge_in: bfloat16 [1024, 512], replicated, may hold values from -0.1875 to 0.1875
- edge_out: bfloat16 [512, 512], replicated, may hold values from -0.25 to 0.25
- node_in: bfloat16 [1024, 512], replicated, may hold values from -0.1875 to 0.1875
- node_out: bfloat16 [512, 512], replicated, may hold values from -0.25 to 0.25
- up_weight: bfloat16 [512, 512], replicated, may hold values from -0.25 to 0.25
- mid_in: bfloat16 [1024, 512], replicated, may hold values from -0.1875 to 0.1875
- mid_out: bfloat16 [512, 512], replicated, may hold values from -0.25 to 0.25
- down_in: bfloat16 [1024, 512], replicated, may hold values from -0.1875 to 0.1875
Outputs:
- fine_out: bfloat16 [98304, 512], P(('grp', 'dev'))
- mid_new: bfloat16 [24576, 512], P(('grp', 'dev'))
The draws below stay inside these ranges and needn't reach their ends.
Inputs may be any that keep to these rules, and one draw needn't show every extreme that they name: `owners`: among the 384 fine nodes of one device, at most 12 name the same owner value, a bound that some block reaches.
All inputs are finite; a program needn't handle non-finite values.
Results may differ from the reference program's by a relative error of at most 0.014.
Values may be sent and summed in bfloat16 or wider, within the bound.
A program may use at most 64 MiB of HBM per device.

```python
import math
import jax
import jax.numpy as jnp
import numpy as np
from jax import lax

D = 512
DEG = 6
FN_DEV = 384
MN_DEV = 96
CAP = 12
NF = 98304
NM = 24576
N_GRP = 4
N_DEV = 64


def plant(array, own_key, low, largest):
    place = [jax.random.randint(jax.random.fold_in(own_key, axis), (), 0, length) for axis, length in enumerate(array.shape)]
    widest = array.shape.index(max(array.shape))
    beside = place[:widest] + [(place[widest] + 1) % array.shape[widest]] + place[widest + 1:]
    return array.at[tuple(place)].set(low).at[tuple(beside)].set(largest)


def level_of(key, extent, split, smallest, high):
    gain = 1.0
    for position, blocks in split:
        heights = jax.random.uniform(jax.random.fold_in(jax.random.fold_in(key, 6), position), (blocks,), jnp.float32, smallest / len(split), high / len(split))
        gain = gain * jnp.repeat(jnp.exp(heights), extent[position] // blocks).reshape((-1,) + (1,) * (len(extent) - 1 - position))
    return gain


def assign_block(stream_key, own, number, rows, number_of, top, bound, skew):
    ranking = jax.random.permutation(stream_key, number_of)
    packed, common = load_shares(number_of, rows * top, bound, skew, True), load_shares(number_of, rows * top, bound, skew, False)
    places = jnp.arange(number_of)

    def named(lengths, offset_by):
        used = int((lengths > 0).sum())
        fixed = max(1, used // 4)
        moved = fixed + (places - fixed + offset_by * (used - fixed)) % max(1, number_of - fixed)
        return jnp.zeros((number_of,), jnp.int32).at[ranking[jnp.where(places < fixed, places, moved)]].set(jnp.asarray(lengths, jnp.int32))

    lengths = jnp.where(number % 4 == 0, named(packed, number // 4), named(common, number - number // 4 - 1))
    mixed = jax.random.permutation(jax.random.fold_in(own, 3), number_of)
    source_of, taker = mixed[0:number_of // 2 * 2:2], mixed[1:number_of // 2 * 2:2]
    slack = jnp.minimum(lengths[source_of] - 1, bound - lengths[taker]) // 2
    slack = jnp.where((source_of == ranking[0]) | (taker == ranking[0]) | (lengths[taker] == 0), 0, jnp.maximum(slack, 0))
    moved = jax.random.randint(jax.random.fold_in(own, 4), (number_of // 2,), 0, 1 << 20) % (slack + 1)
    lengths = lengths.at[source_of].add(-moved).at[taker].add(moved)
    members = jnp.searchsorted(jnp.cumsum(lengths), jnp.arange(rows * top), side="right").astype(jnp.int32)
    listing = members.reshape(top, rows).T
    listing = listing[jax.random.permutation(jax.random.fold_in(own, 1), rows)]
    offset_by = jax.random.randint(jax.random.fold_in(own, 2), (rows, 1), 0, top)
    return jnp.take_along_axis(listing, (jnp.arange(top)[None, :] + offset_by) % top, axis=1)


def load_shares(amount, total, limit, skew, full):
    portions = [(1 << 20) // math.isqrt(rank ** skew) + 1 for rank in range(1, amount + 1)]
    largest = limit if full else min(limit, max(-(-total // amount), total * portions[0] // sum(portions)))
    least = 1 if total - largest >= amount - 1 else 0
    given, surplus = [largest] + [least] * (amount - 1), total - largest - least * (amount - 1)
    while surplus > 0:
        candidates = [i for i in range(1, amount) if given[i] < largest] or [i for i in range(1, amount) if given[i] < limit]
        whole, remaining = sum([portions[i] for i in candidates]), surplus
        for i in candidates:
            more = min(limit - given[i], max(1, remaining * portions[i] // whole), surplus)
            given[i] = given[i] + more
            surplus = surplus - more
    return np.array(given)


def gaussian(own_key, extent, spread, bound, cuts=(), held_as=jnp.bfloat16):
    drawn = spread * jax.random.normal(own_key, extent, jnp.float32)
    if cuts:
        drawn = drawn * level_of(own_key, extent, cuts, -0.22, 0.18)
    return jnp.clip(drawn, -bound, bound).astype(held_as)


def setup_inputs(seed: int = 0) -> dict:
    streams_of = jax.random.split(jax.random.key(seed), 14)
    nodes = gaussian(streams_of[0], (NF, D), 1.0, 6.0, ((0, 256),))
    senders = plant(jax.random.randint(streams_of[1], (NF * DEG,), 0, 3 * FN_DEV), jax.random.fold_in(streams_of[1], 1), 0, (3 * FN_DEV) - 1).astype(jnp.int32)
    mid_nodes = gaussian(streams_of[2], (NM, D), 1.0, 6.0, ((0, 256),))
    owners_keys = jax.random.split(jax.random.fold_in(streams_of[3], 1), NF // FN_DEV)
    owners_turns = jax.random.permutation(jax.random.fold_in(streams_of[3], 3), NF // FN_DEV)
    owners = jax.vmap(lambda own, number: assign_block(jax.random.fold_in(streams_of[3], 2), own, number, FN_DEV, N_DEV, 1, CAP, 2))(owners_keys, owners_turns).reshape((NF, 1))
    slots = plant(jax.random.randint(streams_of[4], (NF,), 0, MN_DEV), jax.random.fold_in(streams_of[4], 1), 0, MN_DEV - 1).astype(jnp.int32)
    edge_in = gaussian(streams_of[5], (2 * D, D), (2 * D) ** -0.5, 0.1875)
    edge_out = gaussian(streams_of[6], (D, D), D ** -0.5, 0.25)
    node_in = gaussian(streams_of[7], (2 * D, D), (2 * D) ** -0.5, 0.1875)
    node_out = gaussian(streams_of[8], (D, D), D ** -0.5, 0.25)
    up_weight = gaussian(streams_of[9], (D, D), D ** -0.5, 0.25)
    mid_in = gaussian(streams_of[10], (2 * D, D), (2 * D) ** -0.5, 0.1875)
    mid_out = gaussian(streams_of[11], (D, D), D ** -0.5, 0.25)
    down_in = gaussian(streams_of[12], (2 * D, D), (2 * D) ** -0.5, 0.1875)
    return dict(nodes=nodes, senders=senders, mid_nodes=mid_nodes, owners=owners, slots=slots, edge_in=edge_in, edge_out=edge_out, node_in=node_in, node_out=node_out, up_weight=up_weight, mid_in=mid_in, mid_out=mid_out, down_in=down_in)


def edge_block(inputs):
    src_ids, block_nodes, all_nodes, edge_in, edge_out = inputs
    src_rows = jnp.take(all_nodes, src_ids, axis=0)
    dst_rows = jnp.repeat(block_nodes, DEG, axis=0)
    paired = jnp.concatenate([src_rows, dst_rows], axis=1)
    edge_hidden = jax.nn.silu(jnp.dot(paired, edge_in, preferred_element_type=jnp.float32)).astype(jnp.bfloat16)
    edge_msg = jnp.dot(edge_hidden, edge_out, preferred_element_type=jnp.float32).astype(jnp.bfloat16)
    return edge_msg.astype(jnp.float32).reshape(FN_DEV, DEG, -1).sum(axis=1)


def reference(nodes, senders, mid_nodes, owners, slots, edge_in, edge_out, node_in, node_out, up_weight, mid_in, mid_out, down_in):
    node_total = nodes.shape[0]
    feat_width = nodes.shape[1]
    device_total = N_GRP * N_DEV
    edge_ids = jnp.arange(node_total * DEG, dtype=jnp.int32)
    home_dev = (edge_ids // DEG) // FN_DEV
    src_ids = jnp.mod(home_dev * FN_DEV + senders - FN_DEV, node_total).astype(jnp.int32)
    src_blocks = src_ids.reshape(device_total, FN_DEV * DEG)
    node_blocks = nodes.reshape(device_total, FN_DEV, feat_width)

    def one_block(pair):
        return edge_block((pair[0], pair[1], nodes, edge_in, edge_out))

    agg = lax.map(one_block, (src_blocks, node_blocks)).reshape(node_total, feat_width).astype(jnp.bfloat16)
    node_hidden = jax.nn.silu(jnp.dot(jnp.concatenate([nodes, agg], axis=1), node_in, preferred_element_type=jnp.float32)).astype(jnp.bfloat16)
    fine_new = (nodes.astype(jnp.float32) + jnp.dot(node_hidden, node_out, preferred_element_type=jnp.float32)).astype(jnp.bfloat16)
    up_msg = jax.nn.silu(jnp.dot(fine_new, up_weight, preferred_element_type=jnp.float32)).astype(jnp.bfloat16)
    node_ids = jnp.arange(node_total, dtype=jnp.int32)
    group_ids = node_ids // (FN_DEV * N_DEV)
    parent_ids = (group_ids * (MN_DEV * N_DEV) + owners[:, 0] * MN_DEV + slots).astype(jnp.int32)
    mid_total = mid_nodes.shape[0]
    up_sum = jax.ops.segment_sum(up_msg.astype(jnp.float32), parent_ids, num_segments=mid_total).astype(jnp.bfloat16)
    mid_hidden = jax.nn.silu(jnp.dot(jnp.concatenate([mid_nodes, up_sum], axis=1), mid_in, preferred_element_type=jnp.float32)).astype(jnp.bfloat16)
    mid_new = (mid_nodes.astype(jnp.float32) + jnp.dot(mid_hidden, mid_out, preferred_element_type=jnp.float32)).astype(jnp.bfloat16)
    parent_rows = jnp.take(mid_new, parent_ids, axis=0)
    downward = jax.nn.silu(jnp.dot(jnp.concatenate([fine_new, parent_rows], axis=1), down_in, preferred_element_type=jnp.float32))
    fine_out = (fine_new.astype(jnp.float32) + downward).astype(jnp.bfloat16)
    return fine_out, mid_new
```

```python
import functools

import jax
import jax.numpy as jnp
from jax import lax
from jax.experimental import pallas as pl
from jax.experimental.pallas import tpu as pltpu
from jax.sharding import PartitionSpec as P

MESH = pl.DeviceIdType.MESH
BOTH = ("grp", "dev")
BF = jnp.bfloat16
F32 = jnp.float32


def silu(x):
    half = 0.5 * x
    return half + half * jnp.tanh(half)


def mm(a, b):
    return jnp.dot(a, b, preferred_element_type=F32)


def hot(match):
    return jnp.where(match, 1.0, 0.0).astype(BF)


def swap4(x):
    return pltpu.roll(x, 4, 1)


def pack(rows, pairs):
    groups = rows.shape[0] // 8
    t = [rows[:, 128 * j : 128 * (j + 1)].reshape(groups, 8, 128) for j in range(4)]
    low = lax.broadcasted_iota(jnp.int32, (groups, 8, 128), 1) < 4
    first = [jnp.where(low, t[j], swap4(t[j + 1])) for j in (0, 2)]
    second = [jnp.where(low, swap4(t[j]), t[j + 1]) for j in (0, 2)]
    first = jnp.concatenate(first, axis=1).astype(BF).reshape(pairs, 1, 3, 16, 128)
    second = jnp.concatenate(second, axis=1).astype(BF).reshape(pairs, 1, 3, 16, 128)
    return jnp.concatenate([first, second], axis=1).reshape(2 * pairs, 3, 16, 128)


def unpack(blocks, pairs):
    both = blocks.astype(F32).reshape(pairs, 2, 3, 16, 128)
    first = both[:, 0].reshape(pairs * 3, 16, 128)
    second = both[:, 1].reshape(pairs * 3, 16, 128)
    low = lax.broadcasted_iota(jnp.int32, (pairs * 3, 8, 128), 1) < 4
    tiles = []
    for half in (slice(0, 8), slice(8, 16)):
        a, b = first[:, half], second[:, half]
        tiles.append(jnp.where(low, a, swap4(b)).reshape(pairs * 24, 128).astype(BF))
        tiles.append(jnp.where(low, swap4(a), b).reshape(pairs * 24, 128).astype(BF))
    return jnp.concatenate(tiles, axis=1)


def pack_hot(rows, pairs):
    g = rows.reshape(pairs, 3, 8, 128)
    g0, g1, g2 = g[:, 0], g[:, 1], g[:, 2]
    low = lax.broadcasted_iota(jnp.int32, (pairs, 8, 128), 1) < 4
    first = jnp.concatenate([jnp.where(low, g0, swap4(g1)), g2], axis=1).astype(BF)
    second = jnp.concatenate([jnp.where(low, swap4(g0), g1), swap4(g2)], axis=1).astype(BF)
    out = jnp.concatenate([first.reshape(pairs, 1, 16, 128), second.reshape(pairs, 1, 16, 128)], axis=1)
    return out.reshape(2 * pairs, 16, 128)


def unpack_hot(blocks, pairs):
    both = blocks.astype(F32).reshape(pairs, 2, 16, 128)
    a, b = both[:, 0], both[:, 1]
    low = lax.broadcasted_iota(jnp.int32, (pairs, 8, 128), 1) < 4
    u0 = jnp.where(low, a[:, 0:8], swap4(b[:, 0:8]))
    u1 = jnp.where(low, swap4(a[:, 0:8]), b[:, 0:8])
    u2 = jnp.where(low, a[:, 8:16], swap4(b[:, 8:16]))
    return jnp.concatenate([u[:, None] for u in (u0, u1, u2)], axis=1).reshape(pairs * 24, 128)


def kernel(
    n_grp, n_dev,
    ints_ref, nodes_ref, mids_ref,
    w_ei, w_eo, w_ni, w_no, w_up, w_mi, w_mo, w_di,
    fine_ref, mid_ref,
    hid_v, proj_v, nodes_v, halo, mids_v, v_ei, v_eo, v_ni, v_no, v_up, v_mi, v_mo, v_di,
    acc, hot_s, hot_r, up_s, up_r, dn_s, dn_r,
    load_sem, halo_send, halo_recv, send_sem, recv_sem,
):
    n, d = nodes_v.shape
    m = mids_v.shape[0]
    pairs = n_dev // 2
    slots = n_dev * 12
    grp, dev = lax.axis_index("grp"), lax.axis_index("dev")
    lin = grp * n_dev + dev
    total = n_grp * n_dev
    nxt, prv = lax.rem(lin + 1, total), lax.rem(lin + total - 1, total)
    next_id = (nxt // n_dev, lax.rem(nxt, n_dev))
    prev_id = (prv // n_dev, lax.rem(prv, n_dev))

    loads = []
    for j, (src, dst) in enumerate((
        (nodes_ref, nodes_v), (w_ei, v_ei), (w_ni, v_ni), (w_eo, v_eo), (w_no, v_no), (w_up, v_up),
        (mids_ref, mids_v), (w_mi, v_mi), (w_mo, v_mo), (w_di, v_di),
    )):
        copy = pltpu.make_async_copy(src, dst, load_sem.at[j])
        copy.start()
        loads.append(copy)
    l_nodes, l_ei, l_ni, l_eo, l_no, l_up, l_mids, l_mi, l_mo, l_di = loads

    barrier = pltpu.get_barrier_semaphore()

    @pl.loop(1, n_dev)
    def _(k):
        pl.semaphore_signal(barrier, inc=1, device_id=(grp, lax.rem(dev + k, n_dev)), device_id_type=MESH)

    pl.semaphore_signal(barrier, inc=1, device_id=next_id, device_id_type=MESH)
    pl.semaphore_signal(barrier, inc=1, device_id=prev_id, device_id_type=MESH)
    pl.semaphore_wait(barrier, n_dev + 1)

    to_next = pltpu.make_async_remote_copy(
        src_ref=nodes_ref, dst_ref=halo.at[0], send_sem=halo_send.at[0], recv_sem=halo_recv.at[0],
        device_id=next_id, device_id_type=MESH)
    to_prev = pltpu.make_async_remote_copy(
        src_ref=nodes_ref, dst_ref=halo.at[1], send_sem=halo_send.at[1], recv_sem=halo_recv.at[1],
        device_id=prev_id, device_id_type=MESH)
    to_next.start()
    to_prev.start()

    def send_all(src, dst, j):
        @pl.loop(1, n_dev)
        def _(k):
            peer = lax.rem(dev + k, n_dev)
            pltpu.make_async_remote_copy(
                src_ref=src.at[peer], dst_ref=dst.at[dev], send_sem=send_sem.at[j], recv_sem=recv_sem.at[j],
                device_id=(grp, peer), device_id_type=MESH).start()

        dst[dev] = src[dev]

    def wait_all(buf, sem):
        part = buf.at[pl.ds(0, n_dev - 1)]
        pltpu.make_async_copy(part, part, sem).wait()

    ints = ints_ref[...]
    by_row = ints.astype(F32).T
    owner_row = by_row[6:7, :]
    owner_hot = hot(lax.broadcasted_iota(jnp.int32, (n_dev, n), 0).astype(F32) == owner_row)
    earlier = hot(lax.broadcasted_iota(jnp.int32, (n, n), 0) < lax.broadcasted_iota(jnp.int32, (n, n), 1))
    before = mm(owner_hot, earlier)
    rank = jnp.sum(before * owner_hot.astype(F32), axis=0, keepdims=True).astype(jnp.int32)
    owner_i = owner_row.astype(jnp.int32)
    place = ((owner_i >> 1) * 3 + (rank >> 2)) * 8 + (owner_i & 1) * 4 + (rank & 3)
    placing_t = hot(lax.broadcasted_iota(jnp.int32, (slots, n), 0) == place)
    slot_hot = hot(lax.broadcasted_iota(jnp.int32, (n, 128), 1) == ints[:, 7:8])
    hot_s[...] = pack_hot(mm(placing_t, slot_hot), pairs)
    send_all(hot_s, hot_r, 0)

    l_nodes.wait()
    l_ei.wait()
    own = nodes_v[...]
    proj_v[0:n, :] = mm(own, v_ei[0:d, :]).astype(BF)
    dst_proj = mm(own, v_ei[d : 2 * d, :])
    lanes = lax.broadcasted_iota(jnp.int32, (n, n), 1)
    for k in range(6):
        acc[k] = dst_proj + mm(hot(lanes + n == ints[:, k : k + 1]), proj_v[0:n, :])
    l_ni.wait()
    node_top = mm(own, v_ni[0:d, :])

    to_next.wait()
    to_prev.wait()
    around = halo[...].reshape(2 * n, d)
    proj_v[n : 3 * n, :] = mm(around, v_ei[0:d, :]).astype(BF)
    part = n // 3

    @pl.loop(0, 3)
    def _(j):
        rows = pl.ds(pl.multiple_of(j * part, part), part)
        lanes = lax.broadcasted_iota(jnp.int32, (part, 2 * n), 1)
        lanes = jnp.where(lanes < n, lanes, lanes + n)
        mine = ints_ref[rows, :]
        hidden = jnp.zeros((part, d), F32)
        for k in range(6):
            hidden = hidden + silu(acc[k, rows, :] + mm(hot(lanes == mine[:, k : k + 1]), proj_v[n : 3 * n, :]))
        hid_v[rows, :] = hidden.astype(BF)

    l_eo.wait()
    agg = mm(hid_v[...], v_eo[...]).astype(BF)
    node_hidden = silu(node_top + mm(agg, v_ni[d : 2 * d, :])).astype(BF)
    l_no.wait()
    fine_new = (own.astype(F32) + mm(node_hidden, v_no[...])).astype(BF)
    l_up.wait()
    up_msg = silu(mm(fine_new, v_up[...])).astype(BF)
    up_s[...] = pack(mm(placing_t, up_msg), pairs)
    send_all(up_s, up_r, 1)

    l_di.wait()
    acc[0] = mm(fine_new, v_di[0:d, :])
    acc[1] = fine_new.astype(F32)
    l_mids.wait()
    l_mi.wait()
    mids = mids_v[...]
    mid_top = mm(mids, v_mi[0:d, :])
    l_mo.wait()
    wait_all(hot_r, recv_sem.at[0])
    wait_all(hot_s, send_sem.at[0])
    got_hot = unpack_hot(hot_r[...], pairs)
    got_hot_t = got_hot.T.astype(BF)[0:m, :]
    got_hot = got_hot.astype(BF)[:, 0:m]
    place_b = jnp.broadcast_to(place.astype(F32), (128, n)).T
    placing = jnp.concatenate(
        [hot(place_b == (lax.broadcasted_iota(jnp.int32, (n, 128), 1) + 128 * j).astype(F32)) for j in range(slots // 128)],
        axis=1)

    wait_all(up_r, recv_sem.at[1])
    up_sum = mm(got_hot_t, unpack(up_r[...], pairs)).astype(BF)
    mid_hidden = silu(mid_top + mm(up_sum, v_mi[d : 2 * d, :])).astype(BF)
    mid_new = (mids.astype(F32) + mm(mid_hidden, v_mo[...])).astype(BF)
    dn_s[...] = pack(mm(got_hot, mid_new), pairs)
    send_all(dn_s, dn_r, 2)
    mid_ref[...] = mid_new
    wait_all(up_s, send_sem.at[1])

    wait_all(dn_r, recv_sem.at[2])
    parents = mm(placing, unpack(dn_r[...], pairs)).astype(BF)
    down = silu(acc[0] + mm(parents, v_di[d : 2 * d, :]))
    fine_ref[...] = (acc[1] + down).astype(BF)
    wait_all(dn_s, send_sem.at[2])


def body(n_grp, n_dev, nodes, senders, mid_nodes, owners, slots, *weights):
    n, d = nodes.shape
    m = mid_nodes.shape[0]
    ints = jnp.concatenate([senders.reshape(n, 6), owners, slots[:, None]], axis=1)
    ints = jnp.pad(ints, ((0, 0), (0, 120)))
    vmem = pl.BlockSpec(memory_space=pltpu.VMEM)
    any_ = pl.BlockSpec(memory_space=pl.ANY)
    block = pltpu.VMEM((n_dev, 3, 16, 128), BF)
    hot_block = pltpu.VMEM((n_dev, 16, 128), BF)
    return pl.pallas_call(
        functools.partial(kernel, n_grp, n_dev),
        out_shape=(jax.ShapeDtypeStruct((n, d), BF), jax.ShapeDtypeStruct((m, d), BF)),
        in_specs=[vmem] + [any_] * (2 + len(weights)),
        out_specs=(vmem, vmem),
        scratch_shapes=[pltpu.VMEM((n, d), BF), pltpu.VMEM((3 * n, d), BF), pltpu.VMEM((n, d), BF), pltpu.VMEM((2, n, d), BF), pltpu.VMEM((m, d), BF)]
        + [pltpu.VMEM(w.shape, BF) for w in weights]
        + [pltpu.VMEM((6, n, d), F32), hot_block, hot_block, block, block, block, block]
        + [
            pltpu.SemaphoreType.DMA((10,)),
            pltpu.SemaphoreType.DMA((2,)),
            pltpu.SemaphoreType.DMA((2,)),
            pltpu.SemaphoreType.DMA((3,)),
            pltpu.SemaphoreType.DMA((3,)),
        ],
        compiler_params=pltpu.CompilerParams(
            collective_id=0, has_side_effects=True, vmem_limit_bytes=48 * 1024 * 1024),
        cost_estimate=pl.CostEstimate(flops=7_000_000_000, bytes_accessed=10_000_000, transcendentals=2_000_000),
        name="sweep",
    )(ints, nodes, mid_nodes, *weights)


def solution(mesh):
    sharded, rows, copied = P(BOTH, None), P(BOTH), P()
    return jax.shard_map(
        functools.partial(body, mesh.shape["grp"], mesh.shape["dev"]),
        mesh=mesh,
        in_specs=(sharded, rows, sharded, sharded, rows) + (copied,) * 8,
        out_specs=(sharded, sharded),
        check_vma=False,
    )
```

```python
import functools

import jax
import jax.numpy as jnp
from jax import lax
from jax.experimental import pallas as pl
from jax.experimental.pallas import tpu as pltpu
from jax.sharding import PartitionSpec as P

MESH = pl.DeviceIdType.MESH
BOTH = ("grp", "dev")
BF = jnp.bfloat16
F32 = jnp.float32


def silu(x):
    half = 0.5 * x
    return half + half * jnp.tanh(half)


def mm(a, b):
    return jnp.dot(a, b, preferred_element_type=F32)


def hot(match):
    return jnp.where(match, 1.0, 0.0).astype(BF)


N_Z, N_Q = 8, 8
ORDER = (0, 7, 1, 6, 2, 5, 3, 4)


def kernel(
    n_grp, n_dev,
    edges_ref, owner_ref, slot_ref, nodes_ref, mids_ref,
    w_ei, w_eo, w_ni, w_no, w_up, w_mi, w_mo, w_di,
    fine_ref, mid_ref,
    parents_v, got_v, got_t, from_v, hid_v, proj_v, nodes_v, halo, mids_v, v_ei, v_eo, v_ni, v_no, v_up, v_mi, v_mo, v_di,
    acc, code_s, code_r, up_s, up_r, dn_s, dn_r, sums, ring_s, ring_r, ag,
    load_sem, halo_send, halo_recv, code_send, code_recv, up_send, up_recv, dn_send, dn_recv,
    rs_send, rs_recv, ag_send, ag_recv,
):
    n, d = nodes_v.shape
    m = mids_v.shape[0]
    grp, dev = lax.axis_index("grp"), lax.axis_index("dev")
    lin = grp * n_dev + dev
    total = n_grp * n_dev
    nxt, prv = lax.rem(lin + 1, total), lax.rem(lin + total - 1, total)
    next_id = (nxt // n_dev, lax.rem(nxt, n_dev))
    prev_id = (prv // n_dev, lax.rem(prv, n_dev))

    loads = []
    for j, (src, dst) in enumerate((
        (nodes_ref, nodes_v), (w_ei, v_ei), (w_ni, v_ni), (w_eo, v_eo), (w_no, v_no), (w_up, v_up),
        (mids_ref, mids_v), (w_mi, v_mi), (w_mo, v_mo), (w_di, v_di),
    )):
        copy = pltpu.make_async_copy(src, dst, load_sem.at[j])
        copy.start()
        loads.append(copy)
    l_nodes, l_ei, l_ni, l_eo, l_no, l_up, l_mids, l_mi, l_mo, l_di = loads

    barrier = pltpu.get_barrier_semaphore()

    core, line = lax.rem(dev, 2), lax.div(dev, 2)
    z, y = lax.rem(line, N_Z), lax.div(line, N_Z)
    q = y * 2 + core

    def at(q_to, z_to):
        return (grp, (lax.div(q_to, 2) * N_Z + z_to) * 2 + lax.rem(q_to, 2))

    ring_id = (at(q, lax.rem(z + 1, N_Z)), at(q, lax.rem(z + N_Z - 1, N_Z)))
    peers = [lax.rem(q + k, N_Q) for k in range(1, N_Q)]
    for other in [at(p, z) for p in peers] + list(ring_id):
        pl.semaphore_signal(barrier, inc=1, device_id=other, device_id_type=MESH)
    pl.semaphore_signal(barrier, inc=1, device_id=next_id, device_id_type=MESH)
    pl.semaphore_signal(barrier, inc=1, device_id=prev_id, device_id_type=MESH)
    pl.semaphore_wait(barrier, N_Q + 3)

    to_next = pltpu.make_async_remote_copy(
        src_ref=nodes_ref, dst_ref=halo.at[0], send_sem=halo_send.at[0], recv_sem=halo_recv.at[0],
        device_id=next_id, device_id_type=MESH)
    to_prev = pltpu.make_async_remote_copy(
        src_ref=nodes_ref, dst_ref=halo.at[1], send_sem=halo_send.at[1], recv_sem=halo_recv.at[1],
        device_id=prev_id, device_id_type=MESH)
    to_next.start()
    to_prev.start()

    def send_all(src, dst, send, recv):
        for p in peers:
            pltpu.make_async_remote_copy(
                src_ref=src.at[p], dst_ref=dst.at[q], send_sem=send, recv_sem=recv,
                device_id=at(p, z), device_id_type=MESH).start()
        dst[q] = src[q]

    def wait_all(buf, sem):
        some = buf.at[pl.ds(0, N_Q - 1)]
        pltpu.make_async_copy(some, some, sem).wait()

    def ring(src, dst, send, recv, way, step, half):
        rows = pl.ds(half * (m // 2), m // 2)
        return pltpu.make_async_remote_copy(
            src_ref=src.at[rows], dst_ref=dst.at[rows],
            send_sem=send.at[way * 4 + step, half], recv_sem=recv.at[way * 4 + step, half],
            device_id=ring_id[way], device_id_type=MESH)

    owner = owner_ref[...]
    ahead = (((owner >> 1) & 7) - z) & 7
    turn = jnp.where(ahead < 4, 2 * ahead, 15 - 2 * ahead)
    owner_q = (owner >> 4) * 2 + (owner & 1)
    block_ids = lax.broadcasted_iota(jnp.int32, (n_dev, n), 0)
    owner_hot = hot(block_ids == turn * 8 + owner_q)
    earlier = hot(lax.broadcasted_iota(jnp.int32, (n, n), 0) < lax.broadcasted_iota(jnp.int32, (n, n), 1))
    before = mm(owner_hot, earlier)
    rank = jnp.sum(before * owner_hot.astype(F32), axis=0, keepdims=True).astype(jnp.int32)
    place = (turn * 8 + owner_q) * 16 + rank
    ranked = jnp.where(lax.broadcasted_iota(jnp.int32, (128, n), 0) == rank, slot_ref[...] + 1, 0)
    ranked = ranked.astype(F32).astype(BF)
    code = lax.dot_general(
        hot(block_ids == owner_q * 8 + turn), ranked, (((1,), (1,)), ((), ())), preferred_element_type=F32)
    code_s[...] = code.reshape(N_Q, 8, 128)
    send_all(code_s, code_r, code_send.at[0], code_recv.at[0])

    flat = edges_ref[...]
    parts = jnp.concatenate([flat >> 5, flat & 31], axis=1).astype(F32).astype(BF)
    lines = flat.shape[0]
    row_ids = lax.broadcasted_iota(jnp.int32, (n, 32), 0)
    line_ids = lax.broadcasted_iota(jnp.int32, (n, 32), 1)
    lane_ids = lax.broadcasted_iota(jnp.int32, (n, 128), 1)
    edge_ids = lax.broadcasted_iota(jnp.int32, (n, 128), 0) * 6
    parts = jnp.concatenate([parts, jnp.zeros((32 - lines, 256), BF)], axis=0)
    for k in range(6):
        line = mm(hot(line_ids == (row_ids * 6 + k) >> 7), parts)
        line = line[:, 0:128] * 32.0 + line[:, 128:256]
        line = jnp.where(lane_ids == ((edge_ids + k) & 127), line, 0.0)
        from_v[:, k : k + 1] = jnp.sum(line, axis=1, keepdims=True).astype(jnp.int32)

    l_nodes.wait()
    l_ei.wait()
    own = nodes_v[...]
    proj_v[0:n, :] = mm(own, v_ei[0:d, :]).astype(BF)
    dst_proj = mm(own, v_ei[d : 2 * d, :])
    ints = from_v[...]
    lanes = lax.broadcasted_iota(jnp.int32, (n, n), 1)
    for k in range(6):
        acc[k] = dst_proj + mm(hot(lanes + n == ints[:, k : k + 1]), proj_v[0:n, :])
    l_ni.wait()
    node_top = mm(own, v_ni[0:d, :])

    wait_all(code_r, code_recv.at[0])
    wait_all(code_s, code_send.at[0])
    got = code_r[...].reshape(n_dev, 128).astype(BF)
    rows = lax.broadcasted_iota(jnp.int32, (16 * n_dev, n_dev), 0)
    line = mm(hot(lax.broadcasted_iota(jnp.int32, (16 * n_dev, n_dev), 1) == ((rows >> 4) & 7) * 8 + (rows >> 7)), got)
    rows = lax.broadcasted_iota(jnp.int32, (16 * n_dev, 128), 0)
    cols = lax.broadcasted_iota(jnp.int32, (16 * n_dev, 128), 1)
    line = jnp.where(cols == (rows & 15), line, 0.0)
    line = jnp.sum(line, axis=1, keepdims=True).astype(jnp.int32) - 1
    got_hot = jnp.where(cols == line, 1.0, 0.0)
    for j in range(8):
        got_t[j] = got_hot[128 * j : 128 * (j + 1)].T.astype(BF)
    got_v[...] = got_hot.astype(BF)

    to_next.wait()
    to_prev.wait()
    around = halo[...].reshape(2 * n, d)
    proj_v[n : 3 * n, :] = mm(around, v_ei[0:d, :]).astype(BF)
    part = n // 3

    @pl.loop(0, 3)
    def _(j):
        rows = pl.ds(pl.multiple_of(j * part, part), part)
        lanes = lax.broadcasted_iota(jnp.int32, (part, 2 * n), 1)
        lanes = jnp.where(lanes < n, lanes, lanes + n)
        mine = from_v[rows, :]
        hidden = jnp.zeros((part, d), F32)
        for k in range(6):
            hidden = hidden + silu(acc[k, rows, :] + mm(hot(lanes == mine[:, k : k + 1]), proj_v[n : 3 * n, :]))
        hid_v[rows, :] = hidden.astype(BF)

    l_eo.wait()
    agg = mm(hid_v[...], v_eo[...]).astype(BF)
    node_hidden = silu(node_top + mm(agg, v_ni[d : 2 * d, :])).astype(BF)
    l_no.wait()
    fine_new = (own.astype(F32) + mm(node_hidden, v_no[...])).astype(BF)
    l_up.wait()
    up_msg = silu(mm(fine_new, v_up[...])).astype(BF)
    slot_ids = lax.broadcasted_iota(jnp.int32, (128, n), 0)
    for j in range(7, -1, -1):
        up_s[j] = mm(hot(slot_ids + 128 * j == place), up_msg).astype(BF).reshape(N_Q, 16, d)
        send_all(up_s.at[j], up_r.at[j], up_send.at[j], up_recv.at[j])

    l_di.wait()
    acc[0] = mm(fine_new, v_di[0:d, :])
    acc[1] = fine_new.astype(F32)
    l_mids.wait()
    l_mi.wait()
    mids = mids_v[...]
    mid_top = mm(mids, v_mi[0:d, :])
    l_mo.wait()
    place_b = jnp.broadcast_to(place.astype(F32), (128, n)).T
    placing = jnp.concatenate(
        [hot(place_b == (lax.broadcasted_iota(jnp.int32, (n, 128), 1) + 128 * j).astype(F32)) for j in range(8)],
        axis=1)

    def gather(j):
        wait_all(up_r.at[j], up_recv.at[j])
        sums[ORDER[j]] = mm(got_t[j][0:m, :], up_r[j].reshape(128, d))

    def pass_on(way, step):
        ahead = 4 - step if way == 0 else 5 + step
        slot = way * 4 + step
        for half in range(2):
            rows = slice(half * (m // 2), (half + 1) * (m // 2))
            value = sums[ahead, rows, :]
            if step > 0:
                ring(ring_s.at[slot - 1], ring_r.at[slot - 1], rs_send, rs_recv, way, step - 1, half).wait_recv()
                value = value + ring_r[slot - 1, rows, :].astype(F32)
            ring_s[slot, rows, :] = value.astype(BF)
            ring(ring_s.at[slot], ring_r.at[slot], rs_send, rs_recv, way, step, half).start()

    gather(7)
    pass_on(0, 0)
    gather(6)
    gather(5)
    pass_on(1, 0)
    pass_on(0, 1)
    gather(4)
    gather(3)
    pass_on(1, 1)
    pass_on(0, 2)
    gather(2)
    gather(1)
    pass_on(1, 2)
    pass_on(0, 3)
    gather(0)
    for half in range(2):
        ring(ring_s.at[6], ring_r.at[6], rs_send, rs_recv, 1, 2, half).wait_recv()
    for half in range(2):
        ring(ring_s.at[3], ring_r.at[3], rs_send, rs_recv, 0, 3, half).wait_recv()
    up_sum = (sums[0] + ring_r[6].astype(F32) + ring_r[3].astype(F32)).astype(BF)
    mid_hidden = silu(mid_top + mm(up_sum, v_mi[d : 2 * d, :])).astype(BF)
    mid_new = (mids.astype(F32) + mm(mid_hidden, v_mo[...])).astype(BF)

    def step_of(way, step):
        return (step and 8 - step, 7 - step) if way == 0 else (step, step + 1)

    def hand_on(way, step, half):
        src, dst = step_of(way, step)
        return ring(ag.at[src], ag.at[dst], ag_send, ag_recv, way, step, half)

    def pick(j):
        picked = mm(got_v[128 * j : 128 * (j + 1), 0:m], ag[ORDER[j]])
        dn_s[j] = picked.astype(BF).reshape(N_Q, 16, d)
        send_all(dn_s.at[j], dn_r.at[j], dn_send.at[j], dn_recv.at[j])

    ag[0] = mid_new
    for half in range(2):
        for way in range(2):
            hand_on(way, 0, half).start()
    pick(0)
    mid_ref[...] = mid_new
    for step in range(4):
        ways = (0, 1) if step < 3 else (0,)
        for half in range(2):
            for way in ways:
                hand_on(way, step, half).wait_recv()
                if step + 1 < (4, 3)[way]:
                    hand_on(way, step + 1, half).start()
        for way in ways:
            pick(2 * step + 1 + way)

    for j in range(4):
        wait_all(dn_r.at[j], dn_recv.at[j])
    parents_v[...] = mm(placing[:, 0:512], dn_r[0:4].reshape(512, d))
    for j in range(4, 8):
        wait_all(dn_r.at[j], dn_recv.at[j])
    parents = (parents_v[...] + mm(placing[:, 512:1024], dn_r[4:8].reshape(512, d))).astype(BF)
    down = silu(acc[0] + mm(parents, v_di[d : 2 * d, :]))
    fine_ref[...] = (acc[1] + down).astype(BF)
    for j in range(8):
        wait_all(up_s.at[j], up_send.at[j])
        wait_all(dn_s.at[j], dn_send.at[j])
    for way in range(2):
        for step in range((4, 3)[way]):
            for half in range(2):
                ring(ring_s.at[way * 4 + step], ring_r.at[way * 4 + step], rs_send, rs_recv, way, step, half).wait_send()
                hand_on(way, step, half).wait_send()


def body(n_grp, n_dev, nodes, senders, mid_nodes, owners, slots, *weights):
    n, d = nodes.shape
    m = mid_nodes.shape[0]
    vmem = pl.BlockSpec(memory_space=pltpu.VMEM)
    any_ = pl.BlockSpec(memory_space=pltpu.HBM)
    block = pltpu.VMEM((8, N_Q, 16, d), BF)
    code = pltpu.VMEM((N_Q, 8, 128), F32)
    return pl.pallas_call(
        functools.partial(kernel, n_grp, n_dev),
        out_shape=(jax.ShapeDtypeStruct((n, d), BF), jax.ShapeDtypeStruct((m, d), BF)),
        in_specs=[vmem] * 3 + [any_] * (2 + len(weights)),
        out_specs=(vmem, vmem),
        scratch_shapes=[pltpu.VMEM((n, d), F32), pltpu.VMEM((16 * n_dev, 128), BF), pltpu.VMEM((8, 128, 128), BF), pltpu.VMEM((n, 128), jnp.int32), pltpu.VMEM((n, d), BF), pltpu.VMEM((3 * n, d), BF), pltpu.VMEM((n, d), BF), pltpu.VMEM((2, n, d), BF), pltpu.VMEM((m, d), BF)]
        + [pltpu.VMEM(w.shape, BF) for w in weights]
        + [pltpu.VMEM((6, n, d), F32), code, code, block, block, block, block]
        + [pltpu.VMEM((8, m, d), F32), pltpu.VMEM((7, m, d), BF), pltpu.VMEM((7, m, d), BF), pltpu.VMEM((8, m, d), BF)]
        + [pltpu.SemaphoreType.DMA((k,)) for k in (10, 2, 2, 1, 1, 8, 8, 8, 8)]
        + [pltpu.SemaphoreType.DMA((7, 2))] * 4,
        compiler_params=pltpu.CompilerParams(
            collective_id=0, has_side_effects=True, vmem_limit_bytes=63 * 1024 * 1024),
        cost_estimate=pl.CostEstimate(flops=7_000_000_000, bytes_accessed=10_000_000, transcendentals=2_000_000),
        name="sweep",
    )(senders.reshape(-1, 128), owners.reshape(1, n), slots.reshape(1, n), nodes, mid_nodes, *weights)


def solution(mesh):
    sharded, rows, copied = P(BOTH, None), P(BOTH), P()
    return jax.shard_map(
        functools.partial(body, mesh.shape["grp"], mesh.shape["dev"]),
        mesh=mesh,
        in_specs=(sharded, rows, sharded, sharded, rows) + (copied,) * 8,
        out_specs=(sharded, sharded),
        check_vma=False,
    )
```

```python
import functools

import jax
import jax.numpy as jnp
from jax import lax
from jax.experimental import pallas as pl
from jax.experimental.pallas import tpu as pltpu
from jax.sharding import PartitionSpec as P

MESH = pl.DeviceIdType.MESH
BOTH = ("grp", "dev")
BF = jnp.bfloat16
F32 = jnp.float32


def silu(x):
    half = 0.5 * x
    return half + half * jnp.tanh(half)


def mm(a, b):
    return jnp.dot(a, b, preferred_element_type=F32)


def hot(match):
    return jnp.where(match, 1.0, 0.0).astype(BF)


def swap4(x):
    return pltpu.roll(x, 4, 1)


def pack(rows, pairs):
    groups = rows.shape[0] // 8
    t = [rows[:, 128 * j : 128 * (j + 1)].reshape(groups, 8, 128) for j in range(4)]
    low = lax.broadcasted_iota(jnp.int32, (groups, 8, 128), 1) < 4
    first = [jnp.where(low, t[j], swap4(t[j + 1])) for j in (0, 2)]
    second = [jnp.where(low, swap4(t[j]), t[j + 1]) for j in (0, 2)]
    first = jnp.concatenate(first, axis=1).astype(BF).reshape(pairs, 1, 3, 16, 128)
    second = jnp.concatenate(second, axis=1).astype(BF).reshape(pairs, 1, 3, 16, 128)
    return jnp.concatenate([first, second], axis=1).reshape(2 * pairs, 3, 16, 128)


def unpack(blocks, pairs):
    both = blocks.astype(F32).reshape(pairs, 2, 3, 16, 128)
    first = both[:, 0].reshape(pairs * 3, 16, 128)
    second = both[:, 1].reshape(pairs * 3, 16, 128)
    low = lax.broadcasted_iota(jnp.int32, (pairs * 3, 8, 128), 1) < 4
    tiles = []
    for piece in (slice(0, 8), slice(8, 16)):
        a, b = first[:, piece], second[:, piece]
        tiles.append(jnp.where(low, a, swap4(b)).reshape(pairs * 24, 128).astype(BF))
        tiles.append(jnp.where(low, swap4(a), b).reshape(pairs * 24, 128).astype(BF))
    return jnp.concatenate(tiles, axis=1)


N_Z, N_Q = 8, 8
ORDER = (0, 7, 1, 6, 2, 5, 3, 4)
PIECES = 3


def kernel(
    n_grp, n_dev,
    edges_ref, owner_ref, slot_ref, nodes_ref, mids_ref,
    w_ei, w_eo, w_ni, w_no, w_up, w_mi, w_mo, w_di,
    fine_ref, mid_ref,
    parents_v, got_v, got_t, from_v, hid_v, proj_v, nodes_v, halo, mids_v, v_ei, v_eo, v_ni, v_no, v_up, v_mi, v_mo, v_di,
    acc, code_s, code_r, up_s, up_r, dn_s, dn_r, sums, ring_s, ring_r, ag,
    load_sem, halo_send, halo_recv, code_send, code_recv, up_send, up_recv, dn_send, dn_recv,
    rs_send, rs_recv, ag_send, ag_recv,
):
    n, d = nodes_v.shape
    m = mids_v.shape[0]
    grp, dev = lax.axis_index("grp"), lax.axis_index("dev")
    lin = grp * n_dev + dev
    total = n_grp * n_dev
    nxt, prv = lax.rem(lin + 1, total), lax.rem(lin + total - 1, total)
    next_id = (nxt // n_dev, lax.rem(nxt, n_dev))
    prev_id = (prv // n_dev, lax.rem(prv, n_dev))

    loads = []
    for j, (src, dst) in enumerate((
        (nodes_ref, nodes_v), (w_ei, v_ei), (w_ni, v_ni), (w_eo, v_eo), (w_no, v_no), (w_up, v_up),
        (mids_ref, mids_v), (w_mi, v_mi), (w_mo, v_mo), (w_di, v_di),
    )):
        copy = pltpu.make_async_copy(src, dst, load_sem.at[j])
        copy.start()
        loads.append(copy)
    l_nodes, l_ei, l_ni, l_eo, l_no, l_up, l_mids, l_mi, l_mo, l_di = loads

    barrier = pltpu.get_barrier_semaphore()

    core, line = lax.rem(dev, 2), lax.div(dev, 2)
    z, y = lax.rem(line, N_Z), lax.div(line, N_Z)
    q = y * 2 + core

    def at(q_to, z_to):
        return (grp, (lax.div(q_to, 2) * N_Z + z_to) * 2 + lax.rem(q_to, 2))

    ring_id = (at(q, lax.rem(z + 1, N_Z)), at(q, lax.rem(z + N_Z - 1, N_Z)))
    peers = [lax.rem(q + k, N_Q) for k in range(1, N_Q)]
    for other in [at(p, z) for p in peers] + list(ring_id):
        pl.semaphore_signal(barrier, inc=1, device_id=other, device_id_type=MESH)
    pl.semaphore_signal(barrier, inc=1, device_id=next_id, device_id_type=MESH)
    pl.semaphore_signal(barrier, inc=1, device_id=prev_id, device_id_type=MESH)
    pl.semaphore_wait(barrier, N_Q + 3)

    to_next = pltpu.make_async_remote_copy(
        src_ref=nodes_ref, dst_ref=halo.at[0], send_sem=halo_send.at[0], recv_sem=halo_recv.at[0],
        device_id=next_id, device_id_type=MESH)
    to_prev = pltpu.make_async_remote_copy(
        src_ref=nodes_ref, dst_ref=halo.at[1], send_sem=halo_send.at[1], recv_sem=halo_recv.at[1],
        device_id=prev_id, device_id_type=MESH)
    to_next.start()
    to_prev.start()

    def send_all(src, dst, send, recv):
        for p in peers:
            pltpu.make_async_remote_copy(
                src_ref=src.at[p], dst_ref=dst.at[q], send_sem=send, recv_sem=recv,
                device_id=at(p, z), device_id_type=MESH).start()
        dst[q] = src[q]

    def wait_all(buf, sem):
        some = buf.at[pl.ds(0, N_Q - 1)]
        pltpu.make_async_copy(some, some, sem).wait()

    def ring(src, dst, send, recv, way, step, piece):
        rows = pl.ds(piece * (m // PIECES), m // PIECES)
        return pltpu.make_async_remote_copy(
            src_ref=src.at[rows], dst_ref=dst.at[rows],
            send_sem=send.at[way * 4 + step, piece], recv_sem=recv.at[way * 4 + step, piece],
            device_id=ring_id[way], device_id_type=MESH)

    owner = owner_ref[...]
    ahead = (((owner >> 1) & 7) - z) & 7
    turn = jnp.where(ahead < 4, 2 * ahead, 15 - 2 * ahead)
    owner_q = (owner >> 4) * 2 + (owner & 1)
    block_ids = lax.broadcasted_iota(jnp.int32, (n_dev, n), 0)
    owner_hot = hot(block_ids == turn * 8 + owner_q)
    earlier = hot(lax.broadcasted_iota(jnp.int32, (n, n), 0) < lax.broadcasted_iota(jnp.int32, (n, n), 1))
    before = mm(owner_hot, earlier)
    rank = jnp.sum(before * owner_hot.astype(F32), axis=0, keepdims=True).astype(jnp.int32)
    place = turn * 96 + ((owner_q >> 1) * 3 + (rank >> 2)) * 8 + (owner_q & 1) * 4 + (rank & 3)
    slot_row = jnp.concatenate([slot_ref[j : j + 1, :] for j in range(n // 128)], axis=1)
    ranked = jnp.where(lax.broadcasted_iota(jnp.int32, (128, n), 0) == rank, slot_row + 1, 0)
    ranked = ranked.astype(F32).astype(BF)
    code = lax.dot_general(
        hot(block_ids == owner_q * 8 + turn), ranked, (((1,), (1,)), ((), ())), preferred_element_type=F32)
    code_s[...] = code.reshape(N_Q, 8, 128)
    send_all(code_s, code_r, code_send.at[0], code_recv.at[0])

    flat = edges_ref[...]
    parts = jnp.concatenate([flat >> 5, flat & 31], axis=1).astype(F32).astype(BF)
    lines = flat.shape[0]
    row_ids = lax.broadcasted_iota(jnp.int32, (n, 32), 0)
    line_ids = lax.broadcasted_iota(jnp.int32, (n, 32), 1)
    lane_ids = lax.broadcasted_iota(jnp.int32, (n, 128), 1)
    edge_ids = lax.broadcasted_iota(jnp.int32, (n, 128), 0) * 6
    parts = jnp.concatenate([parts, jnp.zeros((32 - lines, 256), BF)], axis=0)
    for k in range(6):
        line = mm(hot(line_ids == (row_ids * 6 + k) >> 7), parts)
        line = line[:, 0:128] * 32.0 + line[:, 128:256]
        line = jnp.where(lane_ids == ((edge_ids + k) & 127), line, 0.0)
        from_v[:, k : k + 1] = jnp.sum(line, axis=1, keepdims=True).astype(jnp.int32)

    l_nodes.wait()
    l_ei.wait()
    own = nodes_v[...]
    proj_v[0:n, :] = mm(own, v_ei[0:d, :]).astype(BF)
    dst_proj = mm(own, v_ei[d : 2 * d, :])
    ints = from_v[...]
    lanes = lax.broadcasted_iota(jnp.int32, (n, n), 1)
    for k in range(6):
        acc[k] = dst_proj + mm(hot(lanes + n == ints[:, k : k + 1]), proj_v[0:n, :])
    l_ni.wait()
    node_top = mm(own, v_ni[0:d, :])

    wait_all(code_r, code_recv.at[0])
    wait_all(code_s, code_send.at[0])
    got = code_r[...].reshape(n_dev, 128).astype(BF)
    rows = lax.broadcasted_iota(jnp.int32, (16 * n_dev, n_dev), 0)
    triple = (((rows & 127) >> 3) * 43691) >> 17
    source = (2 * triple + ((rows >> 2) & 1)) * 8 + (rows >> 7)
    line = mm(hot((lax.broadcasted_iota(jnp.int32, (16 * n_dev, n_dev), 1) == source) & ((rows & 127) < 96)), got)
    rows = lax.broadcasted_iota(jnp.int32, (16 * n_dev, 128), 0)
    cols = lax.broadcasted_iota(jnp.int32, (16 * n_dev, 128), 1)
    group = (rows & 127) >> 3
    rank_of = (group - 3 * ((group * 43691) >> 17)) * 4 + (rows & 3)
    line = jnp.where(cols == rank_of, line, 0.0)
    line = jnp.sum(line, axis=1, keepdims=True).astype(jnp.int32) - 1
    got_hot = jnp.where(cols == line, 1.0, 0.0)
    for j in range(8):
        got_t[j] = got_hot[128 * j : 128 * (j + 1)].T.astype(BF)
    got_v[...] = got_hot.astype(BF)

    to_next.wait()
    to_prev.wait()
    around = halo[...].reshape(2 * n, d)
    proj_v[n : 3 * n, :] = mm(around, v_ei[0:d, :]).astype(BF)
    part = n // 3

    @pl.loop(0, 3)
    def _(j):
        rows = pl.ds(pl.multiple_of(j * part, part), part)
        lanes = lax.broadcasted_iota(jnp.int32, (part, 2 * n), 1)
        lanes = jnp.where(lanes < n, lanes, lanes + n)
        mine = from_v[rows, :]
        hidden = jnp.zeros((part, d), F32)
        for k in range(6):
            hidden = hidden + silu(acc[k, rows, :] + mm(hot(lanes == mine[:, k : k + 1]), proj_v[n : 3 * n, :]))
        hid_v[rows, :] = hidden.astype(BF)

    l_eo.wait()
    agg = mm(hid_v[...], v_eo[...]).astype(BF)
    node_hidden = silu(node_top + mm(agg, v_ni[d : 2 * d, :])).astype(BF)
    l_no.wait()
    fine_new = (own.astype(F32) + mm(node_hidden, v_no[...])).astype(BF)
    l_up.wait()
    up_msg = silu(mm(fine_new, v_up[...])).astype(BF)
    slot_ids = lax.broadcasted_iota(jnp.int32, (96, n), 0)
    for j in range(7, -1, -1):
        up_s[j] = pack(mm(hot(slot_ids + 96 * j == place), up_msg), N_Q // 2)
        send_all(up_s.at[j], up_r.at[j], up_send.at[j], up_recv.at[j])

    l_di.wait()
    acc[0] = mm(fine_new, v_di[0:d, :])
    acc[1] = fine_new.astype(F32)
    l_mids.wait()
    l_mi.wait()
    mids = mids_v[...]
    mid_top = mm(mids, v_mi[0:d, :])
    l_mo.wait()
    place_b = jnp.broadcast_to(place.astype(F32), (128, n)).T
    placing = jnp.concatenate(
        [hot(place_b == (lax.broadcasted_iota(jnp.int32, (n, 128), 1) + 128 * j).astype(F32)) for j in range(6)],
        axis=1)

    def gather(j):
        wait_all(up_r.at[j], up_recv.at[j])
        sums[ORDER[j]] = mm(got_t[j][0:m, 0:96], unpack(up_r[j], N_Q // 2))

    def pass_on(way, step):
        ahead = 4 - step if way == 0 else 5 + step
        slot = way * 4 + step
        for piece in range(PIECES):
            rows = slice(piece * (m // PIECES), (piece + 1) * (m // PIECES))
            value = sums[ahead, rows, :]
            if step > 0:
                ring(ring_s.at[slot - 1], ring_r.at[slot - 1], rs_send, rs_recv, way, step - 1, piece).wait_recv()
                value = value + ring_r[slot - 1, rows, :].astype(F32)
            ring_s[slot, rows, :] = value.astype(BF)
            ring(ring_s.at[slot], ring_r.at[slot], rs_send, rs_recv, way, step, piece).start()

    gather(7)
    pass_on(0, 0)
    gather(6)
    gather(5)
    pass_on(1, 0)
    pass_on(0, 1)
    gather(4)
    gather(3)
    pass_on(1, 1)
    pass_on(0, 2)
    gather(2)
    gather(1)
    pass_on(1, 2)
    pass_on(0, 3)
    gather(0)
    for piece in range(PIECES):
        ring(ring_s.at[6], ring_r.at[6], rs_send, rs_recv, 1, 2, piece).wait_recv()
    for piece in range(PIECES):
        ring(ring_s.at[3], ring_r.at[3], rs_send, rs_recv, 0, 3, piece).wait_recv()
    up_sum = (sums[0] + ring_r[6].astype(F32) + ring_r[3].astype(F32)).astype(BF)
    mid_hidden = silu(mid_top + mm(up_sum, v_mi[d : 2 * d, :])).astype(BF)
    mid_new = (mids.astype(F32) + mm(mid_hidden, v_mo[...])).astype(BF)

    def step_of(way, step):
        return (step and 8 - step, 7 - step) if way == 0 else (step, step + 1)

    def hand_on(way, step, piece):
        src, dst = step_of(way, step)
        return ring(ag.at[src], ag.at[dst], ag_send, ag_recv, way, step, piece)

    def pick(j):
        dn_s[j] = pack(mm(got_v[128 * j : 128 * j + 96, 0:m], ag[ORDER[j]]), N_Q // 2)
        send_all(dn_s.at[j], dn_r.at[j], dn_send.at[j], dn_recv.at[j])

    ag[0] = mid_new
    for piece in range(PIECES):
        for way in range(2):
            hand_on(way, 0, piece).start()
    pick(0)
    mid_ref[...] = mid_new
    for step in range(4):
        for piece in range(PIECES):
            for way in range(2):
                if step < 3 or (piece == 2) == way:
                    hand_on(way, step, piece).wait_recv()
                if step < 2 or (step == 2 and (piece == 2) == way):
                    hand_on(way, step + 1, piece).start()
        for way in range(2 if step < 3 else 1):
            pick(2 * step + 1 + way)

    def landed(first, last):
        for j in range(first, last):
            wait_all(dn_r.at[j], dn_recv.at[j])
        return jnp.concatenate([unpack(dn_r[j], N_Q // 2) for j in range(first, last)], axis=0)

    parents_v[...] = mm(placing[:, 0:384], landed(0, 4))
    parents = (parents_v[...] + mm(placing[:, 384:768], landed(4, 8))).astype(BF)
    down = silu(acc[0] + mm(parents, v_di[d : 2 * d, :]))
    fine_ref[...] = (acc[1] + down).astype(BF)
    for j in range(8):
        wait_all(up_s.at[j], up_send.at[j])
        wait_all(dn_s.at[j], dn_send.at[j])
    for way in range(2):
        for step in range((4, 3)[way]):
            for piece in range(PIECES):
                ring(ring_s.at[way * 4 + step], ring_r.at[way * 4 + step], rs_send, rs_recv, way, step, piece).wait_send()
        for step in range(4):
            for piece in range(PIECES):
                if step < 3 or (piece == 2) == way:
                    hand_on(way, step, piece).wait_send()


def body(n_grp, n_dev, nodes, senders, mid_nodes, owners, slots, *weights):
    n, d = nodes.shape
    m = mid_nodes.shape[0]
    vmem = pl.BlockSpec(memory_space=pltpu.VMEM)
    any_ = pl.BlockSpec(memory_space=pltpu.HBM)
    block = pltpu.VMEM((8, N_Q, 3, 16, 128), BF)
    code = pltpu.VMEM((N_Q, 8, 128), F32)
    return pl.pallas_call(
        functools.partial(kernel, n_grp, n_dev),
        out_shape=(jax.ShapeDtypeStruct((n, d), BF), jax.ShapeDtypeStruct((m, d), BF)),
        in_specs=[vmem] * 3 + [any_] * (2 + len(weights)),
        out_specs=(vmem, vmem),
        scratch_shapes=[pltpu.VMEM((n, d), F32), pltpu.VMEM((16 * n_dev, 128), BF), pltpu.VMEM((8, 128, 128), BF), pltpu.VMEM((n, 128), jnp.int32), pltpu.VMEM((n, d), BF), pltpu.VMEM((3 * n, d), BF), pltpu.VMEM((n, d), BF), pltpu.VMEM((2, n, d), BF), pltpu.VMEM((m, d), BF)]
        + [pltpu.VMEM(w.shape, BF) for w in weights]
        + [pltpu.VMEM((6, n, d), F32), code, code, block, block, block, block]
        + [pltpu.VMEM((8, m, d), F32), pltpu.VMEM((7, m, d), BF), pltpu.VMEM((7, m, d), BF), pltpu.VMEM((8, m, d), BF)]
        + [pltpu.SemaphoreType.DMA((k,)) for k in (10, 2, 2, 1, 1, 8, 8, 8, 8)]
        + [pltpu.SemaphoreType.DMA((8, PIECES))] * 4,
        compiler_params=pltpu.CompilerParams(
            collective_id=0, has_side_effects=True, vmem_limit_bytes=63 * 1024 * 1024),
        cost_estimate=pl.CostEstimate(flops=7_000_000_000, bytes_accessed=10_000_000, transcendentals=2_000_000),
        name="sweep",
    )(senders.reshape(-1, 128), owners.reshape(1, n), slots.reshape(n // 128, 128), nodes, mid_nodes, *weights)


def solution(mesh):
    sharded, rows, copied = P(BOTH, None), P(BOTH), P()
    return jax.shard_map(
        functools.partial(body, mesh.shape["grp"], mesh.shape["dev"]),
        mesh=mesh,
        in_specs=(sharded, rows, sharded, sharded, rows) + (copied,) * 8,
        out_specs=(sharded, sharded),
        check_vma=False,
    )
```

```python
import functools

import jax
import jax.numpy as jnp
from jax import lax
from jax.experimental import pallas as pl
from jax.experimental.pallas import tpu as pltpu
from jax.sharding import PartitionSpec as P

MESH = pl.DeviceIdType.MESH
BOTH = ("grp", "dev")
BF = jnp.bfloat16
F32 = jnp.float32


def silu(x):
    half = 0.5 * x
    return half + half * jnp.tanh(half)


def mm(a, b):
    return jnp.dot(a, b, preferred_element_type=F32)


def hot(match):
    return jnp.where(match, 1.0, 0.0).astype(BF)


def swap4(x):
    return pltpu.roll(x, 4, 1)


def pack(rows, pairs):
    groups = rows.shape[0] // 8
    t = [rows[:, 128 * j : 128 * (j + 1)].reshape(groups, 8, 128) for j in range(4)]
    low = lax.broadcasted_iota(jnp.int32, (groups, 8, 128), 1) < 4
    first = [jnp.where(low, t[j], swap4(t[j + 1])) for j in (0, 2)]
    second = [jnp.where(low, swap4(t[j]), t[j + 1]) for j in (0, 2)]
    first = jnp.concatenate(first, axis=1).astype(BF).reshape(pairs, 1, 3, 16, 128)
    second = jnp.concatenate(second, axis=1).astype(BF).reshape(pairs, 1, 3, 16, 128)
    return jnp.concatenate([first, second], axis=1).reshape(2 * pairs, 3, 16, 128)


def unpack(blocks, pairs):
    both = blocks.astype(F32).reshape(pairs, 2, 3, 16, 128)
    first = both[:, 0].reshape(pairs * 3, 16, 128)
    second = both[:, 1].reshape(pairs * 3, 16, 128)
    low = lax.broadcasted_iota(jnp.int32, (pairs * 3, 8, 128), 1) < 4
    tiles = []
    for piece in (slice(0, 8), slice(8, 16)):
        a, b = first[:, piece], second[:, piece]
        tiles.append(jnp.where(low, a, swap4(b)).reshape(pairs * 24, 128).astype(BF))
        tiles.append(jnp.where(low, swap4(a), b).reshape(pairs * 24, 128).astype(BF))
    return jnp.concatenate(tiles, axis=1)


N_Z, N_Q = 8, 8
ORDER = (0, 7, 1, 6, 2, 5, 3, 4)
PIECES = 6


def kernel(
    n_grp, n_dev,
    edges_ref, owner_ref, slot_ref, nodes_ref, mids_ref,
    w_ei, w_eo, w_ni, w_no, w_up, w_mi, w_mo, w_di,
    fine_ref, mid_ref,
    parents_v, got_v, got_t, from_v, hid_v, proj_v, nodes_v, halo, mids_v, v_ei, v_eo, v_ni, v_no, v_up, v_mi, v_mo, v_di,
    acc, code_s, code_r, up_s, up_r, dn_s, dn_r, sums, ring_s, ring_r, ag,
    load_sem, halo_send, halo_recv, code_send, code_recv, up_send, up_recv, dn_send, dn_recv,
    rs_send, rs_recv, ag_send, ag_recv,
):
    n, d = nodes_v.shape
    m = mids_v.shape[0]
    grp, dev = lax.axis_index("grp"), lax.axis_index("dev")
    lin = grp * n_dev + dev
    total = n_grp * n_dev
    nxt, prv = lax.rem(lin + 1, total), lax.rem(lin + total - 1, total)
    next_id = (nxt // n_dev, lax.rem(nxt, n_dev))
    prev_id = (prv // n_dev, lax.rem(prv, n_dev))

    loads = []
    for j, (src, dst) in enumerate((
        (nodes_ref, nodes_v), (w_ei, v_ei), (w_ni, v_ni), (w_eo, v_eo), (w_no, v_no), (w_up, v_up),
        (mids_ref, mids_v), (w_mi, v_mi), (w_mo, v_mo), (w_di, v_di),
    )):
        copy = pltpu.make_async_copy(src, dst, load_sem.at[j])
        copy.start()
        loads.append(copy)
    l_nodes, l_ei, l_ni, l_eo, l_no, l_up, l_mids, l_mi, l_mo, l_di = loads

    barrier = pltpu.get_barrier_semaphore()

    core, line = lax.rem(dev, 2), lax.div(dev, 2)
    z, y = lax.rem(line, N_Z), lax.div(line, N_Z)
    q = y * 2 + core

    def at(q_to, z_to):
        return (grp, (lax.div(q_to, 2) * N_Z + z_to) * 2 + lax.rem(q_to, 2))

    ring_id = (at(q, lax.rem(z + 1, N_Z)), at(q, lax.rem(z + N_Z - 1, N_Z)))
    peers = [lax.rem(q + k, N_Q) for k in range(1, N_Q)]
    for other in [at(p, z) for p in peers] + list(ring_id):
        pl.semaphore_signal(barrier, inc=1, device_id=other, device_id_type=MESH)
    pl.semaphore_signal(barrier, inc=1, device_id=next_id, device_id_type=MESH)
    pl.semaphore_signal(barrier, inc=1, device_id=prev_id, device_id_type=MESH)
    pl.semaphore_wait(barrier, N_Q + 3)

    to_next = pltpu.make_async_remote_copy(
        src_ref=nodes_ref, dst_ref=halo.at[0], send_sem=halo_send.at[0], recv_sem=halo_recv.at[0],
        device_id=next_id, device_id_type=MESH)
    to_prev = pltpu.make_async_remote_copy(
        src_ref=nodes_ref, dst_ref=halo.at[1], send_sem=halo_send.at[1], recv_sem=halo_recv.at[1],
        device_id=prev_id, device_id_type=MESH)
    to_next.start()
    to_prev.start()

    def send_all(src, dst, send, recv):
        for p in peers:
            pltpu.make_async_remote_copy(
                src_ref=src.at[p], dst_ref=dst.at[q], send_sem=send, recv_sem=recv,
                device_id=at(p, z), device_id_type=MESH).start()
        dst[q] = src[q]

    def wait_all(buf, sem):
        some = buf.at[pl.ds(0, N_Q - 1)]
        pltpu.make_async_copy(some, some, sem).wait()

    def ring(src, dst, send, recv, way, step, piece):
        rows = pl.ds(piece * (m // PIECES), m // PIECES)
        return pltpu.make_async_remote_copy(
            src_ref=src.at[rows], dst_ref=dst.at[rows],
            send_sem=send.at[way * 4 + step, piece], recv_sem=recv.at[way * 4 + step, piece],
            device_id=ring_id[way], device_id_type=MESH)

    owner = owner_ref[...]
    ahead = (((owner >> 1) & 7) - z) & 7
    turn = jnp.where(ahead < 4, 2 * ahead, 15 - 2 * ahead)
    owner_q = (owner >> 4) * 2 + (owner & 1)
    block_ids = lax.broadcasted_iota(jnp.int32, (n_dev, n), 0)
    owner_hot = hot(block_ids == turn * 8 + owner_q)
    earlier = hot(lax.broadcasted_iota(jnp.int32, (n, n), 0) < lax.broadcasted_iota(jnp.int32, (n, n), 1))
    before = mm(owner_hot, earlier)
    rank = jnp.sum(before * owner_hot.astype(F32), axis=0, keepdims=True).astype(jnp.int32)
    place = turn * 96 + ((owner_q >> 1) * 3 + (rank >> 2)) * 8 + (owner_q & 1) * 4 + (rank & 3)
    slot_row = jnp.concatenate([slot_ref[j : j + 1, :] for j in range(n // 128)], axis=1)
    ranked = jnp.where(lax.broadcasted_iota(jnp.int32, (128, n), 0) == rank, slot_row + 1, 0)
    ranked = ranked.astype(F32).astype(BF)
    code = lax.dot_general(
        hot(block_ids == owner_q * 8 + turn), ranked, (((1,), (1,)), ((), ())), preferred_element_type=F32)
    code_s[...] = code.reshape(N_Q, 8, 128)
    send_all(code_s, code_r, code_send.at[0], code_recv.at[0])

    flat = edges_ref[...]
    parts = jnp.concatenate([flat >> 5, flat & 31], axis=1).astype(F32).astype(BF)
    lines = flat.shape[0]
    row_ids = lax.broadcasted_iota(jnp.int32, (n, 32), 0)
    line_ids = lax.broadcasted_iota(jnp.int32, (n, 32), 1)
    lane_ids = lax.broadcasted_iota(jnp.int32, (n, 128), 1)
    edge_ids = lax.broadcasted_iota(jnp.int32, (n, 128), 0) * 6
    parts = jnp.concatenate([parts, jnp.zeros((32 - lines, 256), BF)], axis=0)
    for k in range(6):
        line = mm(hot(line_ids == (row_ids * 6 + k) >> 7), parts)
        line = line[:, 0:128] * 32.0 + line[:, 128:256]
        line = jnp.where(lane_ids == ((edge_ids + k) & 127), line, 0.0)
        from_v[:, k : k + 1] = jnp.sum(line, axis=1, keepdims=True).astype(jnp.int32)

    l_nodes.wait()
    l_ei.wait()
    own = nodes_v[...]
    proj_v[0:n, :] = mm(own, v_ei[0:d, :]).astype(BF)
    dst_proj = mm(own, v_ei[d : 2 * d, :])
    ints = from_v[...]
    lanes = lax.broadcasted_iota(jnp.int32, (n, n), 1)
    for k in range(6):
        acc[k] = dst_proj + mm(hot(lanes + n == ints[:, k : k + 1]), proj_v[0:n, :])
    l_ni.wait()
    node_top = mm(own, v_ni[0:d, :])

    wait_all(code_r, code_recv.at[0])
    wait_all(code_s, code_send.at[0])
    got = code_r[...].reshape(n_dev, 128).astype(BF)
    rows = lax.broadcasted_iota(jnp.int32, (16 * n_dev, n_dev), 0)
    triple = (((rows & 127) >> 3) * 43691) >> 17
    source = (2 * triple + ((rows >> 2) & 1)) * 8 + (rows >> 7)
    line = mm(hot((lax.broadcasted_iota(jnp.int32, (16 * n_dev, n_dev), 1) == source) & ((rows & 127) < 96)), got)
    rows = lax.broadcasted_iota(jnp.int32, (16 * n_dev, 128), 0)
    cols = lax.broadcasted_iota(jnp.int32, (16 * n_dev, 128), 1)
    group = (rows & 127) >> 3
    rank_of = (group - 3 * ((group * 43691) >> 17)) * 4 + (rows & 3)
    line = jnp.where(cols == rank_of, line, 0.0)
    line = jnp.sum(line, axis=1, keepdims=True).astype(jnp.int32) - 1
    got_hot = jnp.where(cols == line, 1.0, 0.0)
    for j in range(8):
        got_t[j] = got_hot[128 * j : 128 * (j + 1)].T.astype(BF)
    got_v[...] = got_hot.astype(BF)

    early = 1 - core
    part = n // 3

    def neighbour(side):
        pltpu.make_async_copy(halo.at[side], halo.at[side], halo_recv.at[side]).wait()
        proj_v[n : 2 * n, :] = mm(halo[side], v_ei[0:d, :]).astype(BF)

    neighbour(early)

    @pl.loop(0, 3)
    def _(j):
        rows = pl.ds(pl.multiple_of(j * part, part), part)
        lanes = lax.broadcasted_iota(jnp.int32, (part, n), 1) + early * (2 * n)
        mine = from_v[rows, :]
        for k in range(6):
            acc[k, rows, :] = acc[k, rows, :] + mm(hot(lanes == mine[:, k : k + 1]), proj_v[n : 2 * n, :])

    neighbour(core)

    @pl.loop(0, 3)
    def _(j):
        rows = pl.ds(pl.multiple_of(j * part, part), part)
        lanes = lax.broadcasted_iota(jnp.int32, (part, n), 1) + core * (2 * n)
        mine = from_v[rows, :]
        hidden = jnp.zeros((part, d), F32)
        for k in range(6):
            hidden = hidden + silu(acc[k, rows, :] + mm(hot(lanes == mine[:, k : k + 1]), proj_v[n : 2 * n, :]))
        hid_v[rows, :] = hidden.astype(BF)

    l_eo.wait()
    agg = mm(hid_v[...], v_eo[...]).astype(BF)
    node_hidden = silu(node_top + mm(agg, v_ni[d : 2 * d, :])).astype(BF)
    l_no.wait()
    fine_new = (own.astype(F32) + mm(node_hidden, v_no[...])).astype(BF)
    l_up.wait()
    up_msg = silu(mm(fine_new, v_up[...])).astype(BF)
    slot_ids = lax.broadcasted_iota(jnp.int32, (96, n), 0)
    for j in range(7, -1, -1):
        up_s[j] = pack(mm(hot(slot_ids + 96 * j == place), up_msg), N_Q // 2)
        send_all(up_s.at[j], up_r.at[j], up_send.at[j], up_recv.at[j])

    l_di.wait()
    acc[0] = mm(fine_new, v_di[0:d, :])
    acc[1] = fine_new.astype(F32)
    l_mids.wait()
    l_mi.wait()
    mids = mids_v[...]
    mid_top = mm(mids, v_mi[0:d, :])
    l_mo.wait()
    place_b = jnp.broadcast_to(place.astype(F32), (128, n)).T
    placing = jnp.concatenate(
        [hot(place_b == (lax.broadcasted_iota(jnp.int32, (n, 128), 1) + 128 * j).astype(F32)) for j in range(6)],
        axis=1)

    def gather(j):
        wait_all(up_r.at[j], up_recv.at[j])
        sums[ORDER[j]] = mm(got_t[j][0:m, 0:96], unpack(up_r[j], N_Q // 2))

    def pass_on(way, step):
        ahead = 4 - step if way == 0 else 5 + step
        slot = way * 4 + step
        for piece in range(PIECES):
            rows = slice(piece * (m // PIECES), (piece + 1) * (m // PIECES))
            value = sums[ahead, rows, :]
            if step > 0:
                ring(ring_s.at[slot - 1], ring_r.at[slot - 1], rs_send, rs_recv, way, step - 1, piece).wait_recv()
                value = value + ring_r[slot - 1, rows, :].astype(F32)
            ring_s[slot, rows, :] = value.astype(BF)
            ring(ring_s.at[slot], ring_r.at[slot], rs_send, rs_recv, way, step, piece).start()

    gather(7)
    pass_on(0, 0)
    gather(6)
    gather(5)
    pass_on(1, 0)
    pass_on(0, 1)
    gather(4)
    gather(3)
    pass_on(1, 1)
    pass_on(0, 2)
    gather(2)
    gather(1)
    pass_on(1, 2)
    pass_on(0, 3)
    gather(0)
    for piece in range(PIECES):
        ring(ring_s.at[6], ring_r.at[6], rs_send, rs_recv, 1, 2, piece).wait_recv()
    for piece in range(PIECES):
        ring(ring_s.at[3], ring_r.at[3], rs_send, rs_recv, 0, 3, piece).wait_recv()
    up_sum = (sums[0] + ring_r[6].astype(F32) + ring_r[3].astype(F32)).astype(BF)
    mid_hidden = silu(mid_top + mm(up_sum, v_mi[d : 2 * d, :])).astype(BF)
    mid_new = (mids.astype(F32) + mm(mid_hidden, v_mo[...])).astype(BF)

    def step_of(way, step):
        return (step and 8 - step, 7 - step) if way == 0 else (step, step + 1)

    def hand_on(way, step, piece):
        src, dst = step_of(way, step)
        return ring(ag.at[src], ag.at[dst], ag_send, ag_recv, way, step, piece)

    def pick(j):
        dn_s[j] = pack(mm(got_v[128 * j : 128 * j + 96, 0:m], ag[ORDER[j]]), N_Q // 2)
        send_all(dn_s.at[j], dn_r.at[j], dn_send.at[j], dn_recv.at[j])

    ag[0] = mid_new
    for piece in range(PIECES):
        for way in range(2):
            hand_on(way, 0, piece).start()
    pick(0)
    mid_ref[...] = mid_new
    for step in range(4):
        for piece in range(PIECES):
            for way in range(2):
                if step < 3 or (piece >= 3) == way:
                    hand_on(way, step, piece).wait_recv()
                if step < 2 or (step == 2 and (piece >= 3) == way):
                    hand_on(way, step + 1, piece).start()
        for way in range(2 if step < 3 else 1):
            pick(2 * step + 1 + way)

    def landed(first, last):
        for j in range(first, last):
            wait_all(dn_r.at[j], dn_recv.at[j])
        return jnp.concatenate([unpack(dn_r[j], N_Q // 2) for j in range(first, last)], axis=0)

    parents_v[...] = mm(placing[:, 0:384], landed(0, 4))
    parents = (parents_v[...] + mm(placing[:, 384:768], landed(4, 8))).astype(BF)
    down = silu(acc[0] + mm(parents, v_di[d : 2 * d, :]))
    fine_ref[...] = (acc[1] + down).astype(BF)
    for j in range(8):
        wait_all(up_s.at[j], up_send.at[j])
        wait_all(dn_s.at[j], dn_send.at[j])
    for way in range(2):
        for step in range((4, 3)[way]):
            for piece in range(PIECES):
                ring(ring_s.at[way * 4 + step], ring_r.at[way * 4 + step], rs_send, rs_recv, way, step, piece).wait_send()
        for step in range(4):
            for piece in range(PIECES):
                if step < 3 or (piece >= 3) == way:
                    hand_on(way, step, piece).wait_send()
    to_next.wait_send()
    to_prev.wait_send()


def body(n_grp, n_dev, nodes, senders, mid_nodes, owners, slots, *weights):
    n, d = nodes.shape
    m = mid_nodes.shape[0]
    vmem = pl.BlockSpec(memory_space=pltpu.VMEM)
    any_ = pl.BlockSpec(memory_space=pltpu.HBM)
    block = pltpu.VMEM((8, N_Q, 3, 16, 128), BF)
    code = pltpu.VMEM((N_Q, 8, 128), F32)
    return pl.pallas_call(
        functools.partial(kernel, n_grp, n_dev),
        out_shape=(jax.ShapeDtypeStruct((n, d), BF), jax.ShapeDtypeStruct((m, d), BF)),
        in_specs=[vmem] * 3 + [any_] * (2 + len(weights)),
        out_specs=(vmem, vmem),
        scratch_shapes=[pltpu.VMEM((n, d), F32), pltpu.VMEM((16 * n_dev, 128), BF), pltpu.VMEM((8, 128, 128), BF), pltpu.VMEM((n, 128), jnp.int32), pltpu.VMEM((n, d), BF), pltpu.VMEM((3 * n, d), BF), pltpu.VMEM((n, d), BF), pltpu.VMEM((2, n, d), BF), pltpu.VMEM((m, d), BF)]
        + [pltpu.VMEM(w.shape, BF) for w in weights]
        + [pltpu.VMEM((6, n, d), F32), code, code, block, block, block, block]
        + [pltpu.VMEM((8, m, d), F32), pltpu.VMEM((7, m, d), BF), pltpu.VMEM((7, m, d), BF), pltpu.VMEM((8, m, d), BF)]
        + [pltpu.SemaphoreType.DMA((k,)) for k in (10, 2, 2, 1, 1, 8, 8, 8, 8)]
        + [pltpu.SemaphoreType.DMA((8, PIECES))] * 4,
        compiler_params=pltpu.CompilerParams(
            collective_id=0, has_side_effects=True, vmem_limit_bytes=int(53.75 * 1024) * 1024),
        cost_estimate=pl.CostEstimate(flops=7_000_000_000, bytes_accessed=10_000_000, transcendentals=2_000_000),
        name="sweep",
    )(senders.reshape(-1, 128), owners.reshape(1, n), slots.reshape(n // 128, 128), nodes, mid_nodes, *weights)


def solution(mesh):
    sharded, rows, copied = P(BOTH, None), P(BOTH), P()
    return jax.shard_map(
        functools.partial(body, mesh.shape["grp"], mesh.shape["dev"]),
        mesh=mesh,
        in_specs=(sharded, rows, sharded, sharded, rows) + (copied,) * 8,
        out_specs=(sharded, sharded),
        check_vma=False,
    )
```

```python
import functools

import jax
import jax.numpy as jnp
from jax import lax
from jax.experimental import pallas as pl
from jax.experimental.pallas import tpu as pltpu
from jax.sharding import PartitionSpec as P

MESH = pl.DeviceIdType.MESH
BOTH = ("grp", "dev")
BF = jnp.bfloat16
F32 = jnp.float32


def silu(x):
    half = 0.5 * x
    return half + half * jnp.tanh(half)


def mm(a, b):
    return jnp.dot(a, b, preferred_element_type=F32)


def hot(match):
    return jnp.where(match, 1.0, 0.0).astype(BF)


def swap4(x):
    return pltpu.roll(x, 4, 1)


def pack(rows, pairs):
    groups = rows.shape[0] // 8
    t = [rows[:, 128 * j : 128 * (j + 1)].reshape(groups, 8, 128) for j in range(4)]
    low = lax.broadcasted_iota(jnp.int32, (groups, 8, 128), 1) < 4
    first = [jnp.where(low, t[j], swap4(t[j + 1])) for j in (0, 2)]
    second = [jnp.where(low, swap4(t[j]), t[j + 1]) for j in (0, 2)]
    first = jnp.concatenate(first, axis=1).astype(BF).reshape(pairs, 1, 3, 16, 128)
    second = jnp.concatenate(second, axis=1).astype(BF).reshape(pairs, 1, 3, 16, 128)
    return jnp.concatenate([first, second], axis=1).reshape(2 * pairs, 3, 16, 128)


def unpack(blocks, pairs):
    both = blocks.astype(F32).reshape(pairs, 2, 3, 16, 128)
    first = both[:, 0].reshape(pairs * 3, 16, 128)
    second = both[:, 1].reshape(pairs * 3, 16, 128)
    low = lax.broadcasted_iota(jnp.int32, (pairs * 3, 8, 128), 1) < 4
    tiles = []
    for piece in (slice(0, 8), slice(8, 16)):
        a, b = first[:, piece], second[:, piece]
        tiles.append(jnp.where(low, a, swap4(b)).reshape(pairs * 24, 128).astype(BF))
        tiles.append(jnp.where(low, swap4(a), b).reshape(pairs * 24, 128).astype(BF))
    return jnp.concatenate(tiles, axis=1)


N_Z, N_Q = 8, 8
ORDER = (0, 7, 1, 6, 2, 5, 3, 4)
PIECES = 6


def kernel(
    n_grp, n_dev,
    edges_ref, owner_ref, slot_ref, nodes_ref, mids_ref,
    w_ei, w_eo, w_ni, w_no, w_up, w_mi, w_mo, w_di,
    fine_ref, mid_ref,
    parents_v, got_v, got_t, from_v, hid_v, proj_v, nodes_v, halo, mids_v, v_ei, v_eo, v_ni, v_no, v_up, v_mi, v_mo, v_di,
    acc, code_s, code_r, up_s, up_r, dn_s, dn_r, sums, ring_s, ring_r, ag,
    load_sem, halo_send, halo_recv, code_send, code_recv, up_send, up_recv, dn_send, dn_recv,
    rs_send, rs_recv, ag_send, ag_recv,
):
    n, d = nodes_v.shape
    m = mids_v.shape[0]
    grp, dev = lax.axis_index("grp"), lax.axis_index("dev")
    lin = grp * n_dev + dev
    total = n_grp * n_dev
    nxt, prv = lax.rem(lin + 1, total), lax.rem(lin + total - 1, total)
    next_id = (nxt // n_dev, lax.rem(nxt, n_dev))
    prev_id = (prv // n_dev, lax.rem(prv, n_dev))

    loads = []
    for j, (src, dst) in enumerate((
        (nodes_ref, nodes_v), (w_ei, v_ei), (w_ni, v_ni), (w_eo, v_eo), (w_no, v_no), (w_up, v_up),
        (mids_ref, mids_v), (w_mi, v_mi), (w_mo, v_mo), (w_di, v_di),
    )):
        copy = pltpu.make_async_copy(src, dst, load_sem.at[j])
        copy.start()
        loads.append(copy)
    l_nodes, l_ei, l_ni, l_eo, l_no, l_up, l_mids, l_mi, l_mo, l_di = loads

    barrier = pltpu.get_barrier_semaphore()

    core, line = lax.rem(dev, 2), lax.div(dev, 2)
    z, y = lax.rem(line, N_Z), lax.div(line, N_Z)
    q = y * 2 + core

    def at(q_to, z_to):
        return (grp, (lax.div(q_to, 2) * N_Z + z_to) * 2 + lax.rem(q_to, 2))

    ring_id = (at(q, lax.rem(z + 1, N_Z)), at(q, lax.rem(z + N_Z - 1, N_Z)))
    peers = [lax.rem(q + k, N_Q) for k in range(1, N_Q)]
    for other in [at(p, z) for p in peers] + list(ring_id):
        pl.semaphore_signal(barrier, inc=1, device_id=other, device_id_type=MESH)
    pl.semaphore_signal(barrier, inc=1, device_id=next_id, device_id_type=MESH)
    pl.semaphore_signal(barrier, inc=1, device_id=prev_id, device_id_type=MESH)
    pl.semaphore_wait(barrier, N_Q + 3)

    to_next = pltpu.make_async_remote_copy(
        src_ref=nodes_ref, dst_ref=halo.at[0], send_sem=halo_send.at[0], recv_sem=halo_recv.at[0],
        device_id=next_id, device_id_type=MESH)
    to_prev = pltpu.make_async_remote_copy(
        src_ref=nodes_ref, dst_ref=halo.at[1], send_sem=halo_send.at[1], recv_sem=halo_recv.at[1],
        device_id=prev_id, device_id_type=MESH)
    to_next.start()
    to_prev.start()

    def send_all(src, dst, send, recv):
        for p in peers:
            pltpu.make_async_remote_copy(
                src_ref=src.at[p], dst_ref=dst.at[q], send_sem=send, recv_sem=recv,
                device_id=at(p, z), device_id_type=MESH).start()
        dst[q] = src[q]

    def wait_all(buf, sem):
        some = buf.at[pl.ds(0, N_Q - 1)]
        pltpu.make_async_copy(some, some, sem).wait()

    def ring(src, dst, send, recv, way, step, piece):
        rows = pl.ds(piece * (m // PIECES), m // PIECES)
        return pltpu.make_async_remote_copy(
            src_ref=src.at[rows], dst_ref=dst.at[rows],
            send_sem=send.at[way * 4 + step, piece], recv_sem=recv.at[way * 4 + step, piece],
            device_id=ring_id[way], device_id_type=MESH)

    owner = owner_ref[...]
    ahead = (((owner >> 1) & 7) - z) & 7
    turn = jnp.where(ahead < 4, 2 * ahead, 15 - 2 * ahead)
    owner_q = (owner >> 4) * 2 + (owner & 1)
    block_ids = lax.broadcasted_iota(jnp.int32, (n_dev, n), 0)
    owner_hot = hot(block_ids == turn * 8 + owner_q)
    earlier = hot(lax.broadcasted_iota(jnp.int32, (n, n), 0) < lax.broadcasted_iota(jnp.int32, (n, n), 1))
    before = mm(owner_hot, earlier)
    rank = jnp.sum(before * owner_hot.astype(F32), axis=0, keepdims=True).astype(jnp.int32)
    place = turn * 96 + ((owner_q >> 1) * 3 + (rank >> 2)) * 8 + (owner_q & 1) * 4 + (rank & 3)
    slot_row = jnp.concatenate([slot_ref[j : j + 1, :] for j in range(n // 128)], axis=1)
    ranked = jnp.where(lax.broadcasted_iota(jnp.int32, (128, n), 0) == rank, slot_row + 1, 0)
    ranked = ranked.astype(F32).astype(BF)
    code = lax.dot_general(
        hot(block_ids == owner_q * 8 + turn), ranked, (((1,), (1,)), ((), ())), preferred_element_type=F32)
    code_s[...] = code.reshape(N_Q, 8, 128)
    send_all(code_s, code_r, code_send.at[0], code_recv.at[0])

    flat = edges_ref[...]
    parts = jnp.concatenate([flat >> 5, flat & 31], axis=1).astype(F32).astype(BF)
    lines = flat.shape[0]
    row_ids = lax.broadcasted_iota(jnp.int32, (n, 32), 0)
    line_ids = lax.broadcasted_iota(jnp.int32, (n, 32), 1)
    lane_ids = lax.broadcasted_iota(jnp.int32, (n, 128), 1)
    edge_ids = lax.broadcasted_iota(jnp.int32, (n, 128), 0) * 6
    parts = jnp.concatenate([parts, jnp.zeros((32 - lines, 256), BF)], axis=0)
    for k in range(6):
        line = mm(hot(line_ids == (row_ids * 6 + k) >> 7), parts)
        line = line[:, 0:128] * 32.0 + line[:, 128:256]
        line = jnp.where(lane_ids == ((edge_ids + k) & 127), line, 0.0)
        from_v[:, k : k + 1] = jnp.sum(line, axis=1, keepdims=True).astype(jnp.int32)

    l_nodes.wait()
    l_ei.wait()
    own = nodes_v[...]
    proj_v[0:n, :] = mm(own, v_ei[0:d, :]).astype(BF)
    dst_proj = mm(own, v_ei[d : 2 * d, :])
    ints = from_v[...]
    lanes = lax.broadcasted_iota(jnp.int32, (n, n), 1)
    for k in range(6):
        acc[k] = dst_proj + mm(hot(lanes + n == ints[:, k : k + 1]), proj_v[0:n, :])
    l_ni.wait()
    node_top = mm(own, v_ni[0:d, :])

    wait_all(code_r, code_recv.at[0])
    wait_all(code_s, code_send.at[0])
    got = code_r[...].reshape(n_dev, 128).astype(BF)
    rows = lax.broadcasted_iota(jnp.int32, (16 * n_dev, n_dev), 0)
    triple = (((rows & 127) >> 3) * 43691) >> 17
    source = (2 * triple + ((rows >> 2) & 1)) * 8 + (rows >> 7)
    line = mm(hot((lax.broadcasted_iota(jnp.int32, (16 * n_dev, n_dev), 1) == source) & ((rows & 127) < 96)), got)
    rows = lax.broadcasted_iota(jnp.int32, (16 * n_dev, 128), 0)
    cols = lax.broadcasted_iota(jnp.int32, (16 * n_dev, 128), 1)
    group = (rows & 127) >> 3
    rank_of = (group - 3 * ((group * 43691) >> 17)) * 4 + (rows & 3)
    line = jnp.where(cols == rank_of, line, 0.0)
    line = jnp.sum(line, axis=1, keepdims=True).astype(jnp.int32) - 1
    got_hot = jnp.where(cols == line, 1.0, 0.0)
    for j in range(8):
        got_t[j] = got_hot[128 * j : 128 * (j + 1)].T.astype(BF)
    got_v[...] = got_hot.astype(BF)

    to_next.wait()
    to_prev.wait()
    around = halo[...].reshape(2 * n, d)
    proj_v[n : 3 * n, :] = mm(around, v_ei[0:d, :]).astype(BF)
    part = n // 3

    @pl.loop(0, 3)
    def _(j):
        rows = pl.ds(pl.multiple_of(j * part, part), part)
        lanes = lax.broadcasted_iota(jnp.int32, (part, 2 * n), 1)
        lanes = jnp.where(lanes < n, lanes, lanes + n)
        mine = from_v[rows, :]
        hidden = jnp.zeros((part, d), F32)
        for k in range(6):
            hidden = hidden + silu(acc[k, rows, :] + mm(hot(lanes == mine[:, k : k + 1]), proj_v[n : 3 * n, :]))
        hid_v[rows, :] = hidden.astype(BF)

    l_eo.wait()
    agg = mm(hid_v[...], v_eo[...]).astype(BF)
    node_hidden = silu(node_top + mm(agg, v_ni[d : 2 * d, :])).astype(BF)
    l_no.wait()
    fine_new = (own.astype(F32) + mm(node_hidden, v_no[...])).astype(BF)
    l_up.wait()
    up_msg = silu(mm(fine_new, v_up[...])).astype(BF)
    slot_ids = lax.broadcasted_iota(jnp.int32, (96, n), 0)
    for j in range(7, -1, -1):
        up_s[j] = pack(mm(hot(slot_ids + 96 * j == place), up_msg), N_Q // 2)
        send_all(up_s.at[j], up_r.at[j], up_send.at[j], up_recv.at[j])

    l_di.wait()
    acc[0] = mm(fine_new, v_di[0:d, :])
    acc[1] = fine_new.astype(F32)
    l_mids.wait()
    l_mi.wait()
    mids = mids_v[...]
    mid_top = mm(mids, v_mi[0:d, :])
    l_mo.wait()
    place_b = jnp.broadcast_to(place.astype(F32), (128, n)).T
    placing = jnp.concatenate(
        [hot(place_b == (lax.broadcasted_iota(jnp.int32, (n, 128), 1) + 128 * j).astype(F32)) for j in range(6)],
        axis=1)

    def gather(j):
        wait_all(up_r.at[j], up_recv.at[j])
        sums[ORDER[j]] = mm(got_t[j][0:m, 0:96], unpack(up_r[j], N_Q // 2))

    def pass_on(way, step):
        ahead = 4 - step if way == 0 else 5 + step
        slot = way * 4 + step
        for piece in range(PIECES):
            rows = slice(piece * (m // PIECES), (piece + 1) * (m // PIECES))
            value = sums[ahead, rows, :]
            if step > 0:
                ring(ring_s.at[slot - 1], ring_r.at[slot - 1], rs_send, rs_recv, way, step - 1, piece).wait_recv()
                value = value + ring_r[slot - 1, rows, :].astype(F32)
            ring_s[slot, rows, :] = value.astype(BF)
            ring(ring_s.at[slot], ring_r.at[slot], rs_send, rs_recv, way, step, piece).start()

    gather(7)
    pass_on(0, 0)
    gather(6)
    gather(5)
    pass_on(1, 0)
    pass_on(0, 1)
    gather(4)
    gather(3)
    pass_on(1, 1)
    pass_on(0, 2)
    gather(2)
    gather(1)
    pass_on(1, 2)
    pass_on(0, 3)
    gather(0)
    for piece in range(PIECES):
        ring(ring_s.at[6], ring_r.at[6], rs_send, rs_recv, 1, 2, piece).wait_recv()
    for piece in range(PIECES):
        ring(ring_s.at[3], ring_r.at[3], rs_send, rs_recv, 0, 3, piece).wait_recv()
    up_sum = (sums[0] + ring_r[6].astype(F32) + ring_r[3].astype(F32)).astype(BF)
    mid_hidden = silu(mid_top + mm(up_sum, v_mi[d : 2 * d, :])).astype(BF)
    mid_new = (mids.astype(F32) + mm(mid_hidden, v_mo[...])).astype(BF)

    def step_of(way, step):
        return (step and 8 - step, 7 - step) if way == 0 else (step, step + 1)

    def hand_on(way, step, piece):
        src, dst = step_of(way, step)
        return ring(ag.at[src], ag.at[dst], ag_send, ag_recv, way, step, piece)

    def pick(j):
        dn_s[j] = pack(mm(got_v[128 * j : 128 * j + 96, 0:m], ag[ORDER[j]]), N_Q // 2)
        send_all(dn_s.at[j], dn_r.at[j], dn_send.at[j], dn_recv.at[j])

    ag[0] = mid_new
    for piece in range(PIECES):
        for way in range(2):
            hand_on(way, 0, piece).start()
    pick(0)
    mid_ref[...] = mid_new
    for step in range(4):
        for piece in range(PIECES):
            for way in range(2):
                if step < 3 or (piece >= 3) == way:
                    hand_on(way, step, piece).wait_recv()
                if step < 2 or (step == 2 and (piece >= 3) == way):
                    hand_on(way, step + 1, piece).start()
        for way in range(2 if step < 3 else 1):
            pick(2 * step + 1 + way)

    def landed(first, last):
        for j in range(first, last):
            wait_all(dn_r.at[j], dn_recv.at[j])
        return jnp.concatenate([unpack(dn_r[j], N_Q // 2) for j in range(first, last)], axis=0)

    parents_v[...] = mm(placing[:, 0:384], landed(0, 4))
    parents = (parents_v[...] + mm(placing[:, 384:768], landed(4, 8))).astype(BF)
    down = silu(acc[0] + mm(parents, v_di[d : 2 * d, :]))
    fine_ref[...] = (acc[1] + down).astype(BF)
    for j in range(8):
        wait_all(up_s.at[j], up_send.at[j])
        wait_all(dn_s.at[j], dn_send.at[j])
    for way in range(2):
        for step in range((4, 3)[way]):
            for piece in range(PIECES):
                ring(ring_s.at[way * 4 + step], ring_r.at[way * 4 + step], rs_send, rs_recv, way, step, piece).wait_send()
        for step in range(4):
            for piece in range(PIECES):
                if step < 3 or (piece >= 3) == way:
                    hand_on(way, step, piece).wait_send()


def body(n_grp, n_dev, nodes, senders, mid_nodes, owners, slots, *weights):
    n, d = nodes.shape
    m = mid_nodes.shape[0]
    vmem = pl.BlockSpec(memory_space=pltpu.VMEM)
    any_ = pl.BlockSpec(memory_space=pltpu.HBM)
    block = pltpu.VMEM((8, N_Q, 3, 16, 128), BF)
    code = pltpu.VMEM((N_Q, 8, 128), F32)
    return pl.pallas_call(
        functools.partial(kernel, n_grp, n_dev),
        out_shape=(jax.ShapeDtypeStruct((n, d), BF), jax.ShapeDtypeStruct((m, d), BF)),
        in_specs=[vmem] * 3 + [any_] * (2 + len(weights)),
        out_specs=(vmem, vmem),
        scratch_shapes=[pltpu.VMEM((n, d), F32), pltpu.VMEM((16 * n_dev, 128), BF), pltpu.VMEM((8, 128, 128), BF), pltpu.VMEM((n, 128), jnp.int32), pltpu.VMEM((n, d), BF), pltpu.VMEM((3 * n, d), BF), pltpu.VMEM((n, d), BF), pltpu.VMEM((2, n, d), BF), pltpu.VMEM((m, d), BF)]
        + [pltpu.VMEM(w.shape, BF) for w in weights]
        + [pltpu.VMEM((6, n, d), F32), code, code, block, block, block, block]
        + [pltpu.VMEM((8, m, d), F32), pltpu.VMEM((7, m, d), BF), pltpu.VMEM((7, m, d), BF), pltpu.VMEM((8, m, d), BF)]
        + [pltpu.SemaphoreType.DMA((k,)) for k in (10, 2, 2, 1, 1, 8, 8, 8, 8)]
        + [pltpu.SemaphoreType.DMA((8, PIECES))] * 4,
        compiler_params=pltpu.CompilerParams(
            collective_id=0, has_side_effects=True, vmem_limit_bytes=63 * 1024 * 1024),
        cost_estimate=pl.CostEstimate(flops=7_000_000_000, bytes_accessed=10_000_000, transcendentals=2_000_000),
        name="sweep",
    )(senders.reshape(-1, 128), owners.reshape(1, n), slots.reshape(n // 128, 128), nodes, mid_nodes, *weights)


def solution(mesh):
    sharded, rows, copied = P(BOTH, None), P(BOTH), P()
    return jax.shard_map(
        functools.partial(body, mesh.shape["grp"], mesh.shape["dev"]),
        mesh=mesh,
        in_specs=(sharded, rows, sharded, sharded, rows) + (copied,) * 8,
        out_specs=(sharded, sharded),
        check_vma=False,
    )
```
